128 devices in a mesh: fit: 8 (over x, core), pair: 16 (over z, y).
Axes of the slice: x: 4, y: 4, z: 4, core: 2. Of those that a mesh axis runs over, the one named last changes fastest.
Arguments:
- ints: bfloat16 [2048, 8, 128, 128], P(('fit', 'pair')), may hold values from -6 to 6
- tile_mu: int32 [2048], P(('fit', 'pair')), may hold values from 0 to 15
- tile_lam: int32 [2048], P(('fit', 'pair')), may hold values from 0 to 15
- tile_live: int32 [2048], P(('fit', 'pair')), may hold values 0 or 1
- coefficients: bfloat16 [2048, 1024], replicated, may hold values from -0.5 to 0.5
- occ_ids: int32 [2], replicated, may hold values from 0 to 7
Outputs:
- exchange: float32 [2048, 2048], P('pair', 'fit')
The draws below stay inside these ranges and needn't reach their ends.
All inputs are finite; a program needn't handle non-finite values. No bound on the sum of `tile_live` on one device may be relied on, other than what follows from the above.
Results may differ from the reference program's by a relative error of at most 0.00045.
Values sent between devices are 32-bit elements; how exact they have to be, the bound alone decides.
No kernel may reach another device: no remote copies, remote signals or barrier semaphores. Data moves between devices by JAX's collectives and lax.ppermute only.
A program may use at most 256 MiB of HBM per device.

```python
import math
import jax
import jax.numpy as jnp
from jax import lax

BT = 128
OCC = 128
NOCC_BLOCKS = 8
OBLK = 2
P_DEV = 8
NT = 16
ROWT = 1
NBT = 16
NBAS = 2048
NTALL = 2048
NOCC_ALL = 1024
N_FIT = 8
N_PAIR = 16


def plant(values, own_key, least, high):
    place = [jax.random.randint(jax.random.fold_in(own_key, axis), (), 0, length) for axis, length in enumerate(values.shape)]
    widest = values.shape.index(max(values.shape))
    neighbour = place[:widest] + [(place[widest] + 1) % values.shape[widest]] + place[widest + 1:]
    return values.at[tuple(place)].set(least).at[tuple(neighbour)].set(high)


def level_of(rng, shape, split, smallest, high):
    def one(axis_at, parts):
        draws = jax.random.uniform(jax.random.fold_in(jax.random.fold_in(rng, 6), axis_at), (parts,), jnp.float32, smallest / len(split), high / len(split))
        return jnp.repeat(jnp.exp(draws), shape[axis_at] // parts).reshape((-1,) + (1,) * (len(shape) - axis_at - 1))

    factor_of = one(*split[0])
    for cut in split[1:]:
        factor_of = factor_of * one(*cut)
    return factor_of


def bell_draw(key, extent, spread, most, pieces=(), kind=jnp.bfloat16):
    result = spread * jax.random.normal(key, extent, jnp.float32)
    if pieces:
        result = result * level_of(key, extent, pieces, -0.22, 0.18)
    return jnp.clip(result, -most, most).astype(kind)


def setup_inputs(seed: int = 0) -> dict:
    splits = jax.random.split(jax.random.key(seed), 7)
    ints = bell_draw(splits[0], (NTALL, P_DEV, BT, BT), 1.0, 6.0, ((0, 128),))
    tile_mu = plant(jax.random.randint(splits[1], (NTALL,), 0, NBT), jax.random.fold_in(splits[1], 1), 0, NBT - 1).astype(jnp.int32)
    tile_lam = plant(jax.random.randint(splits[2], (NTALL,), 0, NBT), jax.random.fold_in(splits[2], 1), 0, NBT - 1).astype(jnp.int32)
    tile_live = plant((jax.random.randint(splits[3], (NTALL,), 0, 4) < 3).astype(jnp.int32), jax.random.fold_in(splits[3], 1), 0, 1)
    coefficients = bell_draw(splits[4], (NBAS, NOCC_ALL), BT ** -0.5, 0.5)
    occ_ids = jax.random.randint(splits[5], (OBLK,), 0, NOCC_BLOCKS).astype(jnp.int32)
    return {"ints": ints, "tile_mu": tile_mu, "tile_lam": tile_lam, "tile_live": tile_live, "coefficients": coefficients, "occ_ids": occ_ids}


def reference(ints, tile_mu, tile_lam, tile_live, coefficients, occ_ids):
    devices = N_FIT * N_PAIR
    basis_tiles = N_PAIR * ROWT
    basis_count = basis_tiles * BT
    k_scale = 1.0 / math.sqrt(devices * P_DEV * OCC * OBLK)
    ints_all = ints.reshape(devices, NT, P_DEV, BT, BT)
    mu_all = tile_mu.reshape(devices, NT)
    lam_all = tile_lam.reshape(devices, NT)
    live_all = tile_live.reshape(devices, NT)
    cblocks = []
    for occ_block in range(OBLK):
        first_col = (occ_ids[occ_block] * OCC).astype(jnp.int32)
        cblock = lax.dynamic_slice_in_dim(coefficients, first_col, OCC, 1)
        cblocks.append(cblock.reshape(basis_tiles, BT, OCC))

    def device_term(summed, carried):
        tile_data, mu_ids, lam_ids, live_flags = carried
        positions = jnp.arange(basis_tiles, dtype=jnp.int32)
        onehot = (mu_ids[:, None] == positions[None, :]).astype(jnp.float32) * live_flags[:, None].astype(jnp.float32)
        for cblock in cblocks:
            lam_rows = cblock[lam_ids]
            products = jnp.einsum('tpml,tli->tpmi', tile_data.astype(jnp.float32), lam_rows.astype(jnp.float32))
            half_block = jnp.einsum('tn,tpmi->pnmi', onehot, products, precision=lax.Precision.HIGHEST)
            half_block = half_block.astype(jnp.bfloat16).reshape(P_DEV, basis_count, OCC).astype(jnp.float32)
            summed = summed + jnp.einsum('pmi,pni->mn', half_block, half_block)
        return (summed, None)
    initial = jnp.zeros((basis_count, basis_count), jnp.float32)
    summed, unused = lax.scan(device_term, initial, (ints_all, mu_all, lam_all, live_all))
    return summed * k_scale
```

```python
import functools
import math

import jax
import jax.numpy as jnp
from jax import lax
from jax.experimental import pallas as pl
from jax.experimental.pallas import tpu as pltpu
from jax.sharding import PartitionSpec as P

OCC = 128
OBLK = 2
BT = 128
EXTRA = 8
COLOURS = ((0, 24), (24, 48), (48, 72), (72, 104), (104, 128))
AXES = ("fit", "pair")
NDEV = 128
SHARES = NDEV // 2
PARTS = len(COLOURS)
KERNEL_VMEM = 28 * 1024 * 1024
LIST = 32
PARTNERS = ((), (1,), (0,), (0, 1))


def coords(index):
    return index >> 5, (index >> 4) & 1, (index >> 2) & 3, index & 3


def index_of(x, core, z, y):
    return (x << 5) | (core << 4) | (z << 2) | y


def flipped(index, axes, second):
    x, core, z, y = coords(index)
    flip = 3 if (core == 1) != second else 1
    place = [x, z, y]
    for axis in axes:
        place[axis] ^= flip
    return index_of(place[0], core, place[1], place[2])


def axis_pairs(axes, second):
    return [(index, flipped(index, axes, second)) for index in range(NDEV)]


def core_pairs():
    return [(index, index ^ 16) for index in range(NDEV)]


def mirror(index):
    x, core, z, y = coords(index)
    row, col = z * 4 + y, x * 2 + core
    high = row >> 1
    if high < col:
        row, col = 2 * col + (row & 1), high
    elif high > col:
        row, col = 2 * col + 1 - (row & 1), high
    else:
        row ^= 1
    return index_of(col >> 1, col & 1, row >> 2, row & 3)


def bits_of(r, core):
    top, mixed = r >> 1, (r >> 1) ^ (r & 1)
    return jnp.where(core == 0, mixed, top), jnp.where(core == 0, top, mixed)


def row_place(row, core, my_z, my_y):
    z_high, z_low = bits_of((row >> 2) ^ my_z, core)
    y_high, y_low = bits_of((row & 3) ^ my_y, core)
    return z_high * 16 + y_high * 8 + z_low * 2 + y_low


def col_place(col, my_x):
    x_high, x_low = bits_of((col >> 1) ^ my_x, col & 1)
    return x_high * 32 + x_low * 4


def my_place():
    fit, pair = lax.axis_index("fit"), lax.axis_index("pair")
    return fit >> 1, fit & 1, pair >> 2, pair & 3


def packed_place(pair, me):
    my_x, _, my_z, my_y = me
    return row_place(2 * pair + 1, pair & 1, my_z, my_y) + col_place(pair, my_x)


def partial_kernel(mu_hbm, lam_hbm, live_hbm, occ_hbm, ints, coeff, *refs):
    keeps, sends, refs = refs[:PARTS], refs[PARTS : 2 * PARTS], refs[2 * PARTS :]
    (
        ints_v, coeff_v, acc, half, diag, info, mu, lam, live, occ,
        order, first, count, place, ints_sem, coeff_sem, small_sem,
    ) = refs
    slots, fitting = ints.shape[0], ints.shape[1]
    tiles = coeff.shape[0] // BT
    me = my_place()
    my_x, my_core, my_z, my_y = me

    def coeff_copy(b):
        start = pl.multiple_of(occ[b] * OCC, OCC)
        return pltpu.make_async_copy(
            coeff.at[:, pl.ds(start, OCC)], coeff_v.at[:, pl.ds(b * OCC, OCC)], coeff_sem.at[b]
        )

    def ints_copy(t):
        return pltpu.make_async_copy(ints.at[t], ints_v.at[t], ints_sem.at[t])

    small = [
        pltpu.make_async_copy(source, target, small_sem.at[i])
        for i, (source, target) in enumerate(((occ_hbm, occ), (mu_hbm, mu), (live_hbm, live), (lam_hbm, lam)))
    ]
    for copy in small:
        copy.start()
    small[0].wait()
    for b in range(OBLK):
        coeff_copy(b).start()
    for copy in small[1:]:
        copy.wait()

    for m in range(tiles):
        place[m] = 0
    for t in range(slots):
        place[mu[t]] = place[mu[t]] + live[t]
    n_slots, n_tiles = jnp.int32(0), jnp.int32(0)
    for m in range(tiles):
        here = place[m]
        info[n_tiles] = m
        first[n_tiles] = n_slots
        count[n_tiles] = here
        place[m] = n_slots
        n_slots = n_slots + here
        n_tiles = n_tiles + (here > 0).astype(jnp.int32)
    for t in range(slots):
        at = place[mu[t]]
        order[jnp.where(live[t] == 1, at, LIST - 1)] = t
        place[mu[t]] = at + live[t]

    def fetch(s, carry):
        ints_copy(order[s]).start()
        return carry

    lax.fori_loop(0, n_slots, fetch, 0)
    for r in range(tiles):
        name = jnp.where(r < n_tiles, info[r], 0)
        info[r] = name
        info[LIST + r] = row_place(name, 0, my_z, my_y)
        info[2 * LIST + r] = row_place(name, 1, my_z, my_y)
        info[3 * LIST + r] = col_place(name >> 1, my_x)

    for ref in keeps + sends + (diag,):
        ref[...] = jnp.zeros_like(ref)
    for b in range(OBLK):
        coeff_copy(b).wait()

    def coeff_rows(t):
        return coeff_v[pl.ds(pl.multiple_of(lam[t] * BT, BT), BT), :]

    def one_tile(r):
        start, many = first[r], count[r]
        one = order[start]
        two = order[start + jnp.where(many > 1, 1, 0)]
        left = jnp.concatenate(
            [ints_v[one].reshape(fitting * BT, BT), ints_v[two].reshape(fitting * BT, BT)], axis=1
        )
        rows = coeff_rows(two)
        right = jnp.concatenate(
            [coeff_rows(one), jnp.where(many > 1, rows, jnp.zeros_like(rows))], axis=0
        )
        value = jnp.dot(left, right, preferred_element_type=jnp.float32)
        for p in range(fitting):
            half[r, :, pl.ds(p * OBLK * OCC, OBLK * OCC)] = value[p * BT : (p + 1) * BT].astype(half.dtype)

    def crowded_tile(r):
        acc[...] = jnp.zeros_like(acc)

        def add(s, carry):
            t = order[s]
            acc[...] += jnp.dot(
                ints_v[t].reshape(fitting * BT, BT), coeff_rows(t), preferred_element_type=jnp.float32
            )
            return carry

        lax.fori_loop(first[r], first[r] + count[r], add, 0)
        for p in range(fitting):
            half[r, :, pl.ds(p * OBLK * OCC, OBLK * OCC)] = acc[pl.ds(p * BT, BT), :].astype(half.dtype)

    def tile_pair(k, carry):
        ranks = (2 * k, jnp.minimum(2 * k + 1, n_tiles - 1))

        def arrive(s, inner):
            ints_copy(order[s]).wait()
            return inner

        lax.fori_loop(first[ranks[0]], first[ranks[1]] + count[ranks[1]], arrive, 0)
        for r in ranks:
            one_tile(r)
        for r in ranks:

            @pl.when(count[r] > 2)
            def _():
                crowded_tile(r)

        return carry

    lax.fori_loop(0, (n_tiles + 1) >> 1, tile_pair, 0)

    keep_spare, send_spare = packed_place(my_core, me), packed_place(1 - my_core, me)

    def strip(v):
        left = half[0 : 2 * v + 2].reshape((2 * v + 2) * BT, half.shape[2])
        right = half[2 * v : 2 * v + 2].reshape(2 * BT, half.shape[2])
        value = lax.dot_general(left, right, (((1,), (1,)), ((), ())), preferred_element_type=jnp.float32)
        for j in (2 * v, 2 * v + 1):
            b, valid = info[j], j < n_tiles
            cols = slice((j - 2 * v) * BT, (j - 2 * v + 1) * BT)
            for i in range(j):
                a = info[i]
                mixed = ((a >> 1) != (b >> 1)) & (((a ^ b) & 1) == 1)
                row_rank, col_rank = jnp.where(mixed, j, i), jnp.where(mixed, i, j)
                core = (jnp.where(mixed, a, b) >> 1) & 1
                target = info[LIST * (1 + core) + row_rank] + info[3 * LIST + col_rank]
                keep_at = jnp.where(valid & (core == my_core), target, keep_spare)
                send_at = jnp.where(valid & (core != my_core), target, send_spare)
                for (start, end), keep, send in zip(COLOURS, keeps, sends):
                    block = value[i * BT + start : i * BT + end, cols]
                    keep[keep_at, 0 : end - start, :] = block
                    send[send_at, 0 : end - start, :] = block
            diag[jnp.where(valid, b, tiles)] = value[j * BT : (j + 1) * BT, cols]

    for v in range(tiles // 2):
        pl.when(2 * v < n_tiles)(functools.partial(strip, v))

    at_row = lax.broadcasted_iota(jnp.int32, (BT, BT), 0)
    at_col = lax.broadcasted_iota(jnp.int32, (BT, BT), 1)
    for pair in range(tiles // 2):
        even, odd = diag[2 * pair], diag[2 * pair + 1]
        packed = jnp.where(at_row <= at_col, even, odd)
        line = jnp.sum(jnp.where(at_row == at_col, odd, 0.0), axis=0, keepdims=True)
        packed = jnp.concatenate([packed, jnp.broadcast_to(line, (EXTRA, BT))], axis=0)
        target = packed_place(pair, me)
        for ours, refs in ((True, keeps), (False, sends)):

            @pl.when((my_core == pair & 1) == ours)
            def _():
                for (start, end), ref in zip(COLOURS, refs):
                    ref[target] = packed[start : start + ref.shape[1]]


def held(array, space):
    return pltpu.with_memory_space_constraint(array, space)


def partial_sums(ints, tile_mu, tile_lam, tile_live, coefficients, occ_ids):
    slots, fitting = ints.shape[0], ints.shape[1]
    tiles = coefficients.shape[0] // BT
    hbm = pl.BlockSpec(memory_space=pltpu.HBM)
    vmem = pl.BlockSpec(memory_space=pltpu.VMEM)
    shares = [
        pltpu.VMEM((SHARES, end - start + (EXTRA if end == BT else 0), BT), jnp.float32)
        for start, end in COLOURS
    ]
    listed = pltpu.SMEM((LIST,), jnp.int32)
    out = pl.pallas_call(
        partial_kernel,
        out_shape=shares + shares,
        in_specs=[hbm] * 6,
        out_specs=[vmem] * (2 * PARTS),
        scratch_shapes=[
            pltpu.VMEM(ints.shape, ints.dtype),
            pltpu.VMEM((coefficients.shape[0], OBLK * OCC), coefficients.dtype),
            pltpu.VMEM((fitting * BT, OBLK * OCC), jnp.float32),
            pltpu.VMEM((tiles, BT, fitting * OBLK * OCC), jnp.bfloat16),
            pltpu.VMEM((tiles + 1, BT, BT), jnp.float32),
            pltpu.SMEM((4 * LIST,), jnp.int32),
            pltpu.SMEM(tile_mu.shape, jnp.int32),
            pltpu.SMEM(tile_lam.shape, jnp.int32),
            pltpu.SMEM(tile_live.shape, jnp.int32),
            pltpu.SMEM(occ_ids.shape, jnp.int32),
            listed,
            listed,
            listed,
            listed,
            pltpu.SemaphoreType.DMA((slots,)),
            pltpu.SemaphoreType.DMA((OBLK,)),
            pltpu.SemaphoreType.DMA((4,)),
        ],
        compiler_params=pltpu.CompilerParams(vmem_limit_bytes=KERNEL_VMEM),
        cost_estimate=pl.CostEstimate(flops=8 * 10**9, bytes_accessed=5 * 2**20, transcendentals=0),
        name="partial_sums",
    )(*[held(v, pltpu.HBM) for v in (tile_mu, tile_lam, tile_live, occ_ids, ints, coefficients)])
    return out[:PARTS], out[PARTS:]


def finish_kernel(mine, theirs, out, *, scale):
    fit, pair = lax.axis_index("fit"), lax.axis_index("pair")
    high, odd = pair >> 1, pair & 1
    own = lambda: mine[0:BT, :] * scale
    other = lambda: theirs[...] * scale

    @pl.when(high < fit)
    def _():
        for number in range(2):

            @pl.when(odd == number)
            def _():
                out[:, pl.ds(number * BT, BT)] = own()
                out[:, pl.ds((1 - number) * BT, BT)] = other()

    @pl.when(high > fit)
    def _():
        for number in range(2):

            @pl.when(odd == number)
            def _():
                out[:, pl.ds((1 - number) * BT, BT)] = own().T
                out[:, pl.ds(number * BT, BT)] = other().T

    @pl.when(high == fit)
    def _():
        rows = lax.broadcasted_iota(jnp.int32, (BT, BT), 0)
        cols = lax.broadcasted_iota(jnp.int32, (BT, BT), 1)

        @pl.when(odd == 0)
        def _():
            packed = other()
            out[:, 0:BT] = jnp.where(rows <= cols, packed, packed.T)
            out[:, BT:] = own()

        @pl.when(odd == 1)
        def _():
            line = mine[BT : BT + 1, :] * scale
            filled = jnp.where(rows == cols, line, own())
            out[:, 0:BT] = other().T
            out[:, BT:] = jnp.where(rows >= cols, filled, filled.T)


def on_device(ints, tile_mu, tile_lam, tile_live, coefficients, occ_ids):
    count = lax.axis_size("fit") * lax.axis_size("pair")
    scale = 1.0 / math.sqrt(count * ints.shape[1] * OCC * OBLK)

    def swap(array, pairs):
        return lax.ppermute(array, AXES, pairs)

    def after(array, *others):
        return lax.optimization_barrier((array, *others))[0]

    first_bits = (2, 2, 2, NDEV // 16)
    keeps, sends = partial_sums(ints, tile_mu, tile_lam, tile_live, coefficients, occ_ids)
    keeps = [v.reshape(first_bits + v.shape[1:]) for v in keeps]
    cames = [swap(v, core_pairs()).reshape(first_bits + v.shape[1:]) for v in sends]
    tie = ()
    for step in range(3):
        for number in range(PARTS):
            axis = (number + step) % 3
            theirs = after(cames[number], *tie)
            at = lambda v, bit: lax.index_in_dim(v, bit, axis, keepdims=True)
            out_going = at(keeps[number], 1) + at(theirs, 1)
            keeps[number] = at(keeps[number], 0) + at(theirs, 0)
            cames[number] = swap(out_going, axis_pairs((axis,), False))
            tie = (out_going,)
    merged = []
    for mine, theirs in zip(keeps, cames):
        mine = (mine + after(theirs, *tie)).reshape((4, 2) + mine.shape[-2:])
        merged.append(mine)
        tie = (mine,)
    mine = jnp.concatenate(merged, axis=2)

    came = [swap(mine[b], axis_pairs(PARTNERS[b], True)) for b in (3, 2, 1)]
    mine = mine[0] + came[0] + came[1] + came[2]
    own = mine[0] + swap(mine[1], axis_pairs((2,), True))
    other = swap(own[0:BT], [(i, mirror(i)) for i in range(NDEV)])
    return pl.pallas_call(
        functools.partial(finish_kernel, scale=scale),
        out_shape=jax.ShapeDtypeStruct((BT, 2 * BT), jnp.float32),
        name="finish",
    )(held(own, pltpu.VMEM), held(other, pltpu.VMEM))


def solution(mesh):
    return jax.shard_map(
        on_device,
        mesh=mesh,
        in_specs=(
            P(("fit", "pair"), None, None, None),
            P(("fit", "pair")),
            P(("fit", "pair")),
            P(("fit", "pair")),
            P(),
            P(),
        ),
        out_specs=P("pair", "fit"),
        check_vma=False,
    )
```

```python
import functools
import math

import jax
import jax.numpy as jnp
from jax import lax
from jax.experimental import pallas as pl
from jax.experimental.pallas import tpu as pltpu
from jax.sharding import PartitionSpec as P

OCC = 128
OBLK = 2
BT = 128
EXTRA = 8
COLOURS = ((0, 24), (24, 48), (48, 72), (72, 104), (104, 128))
AXES = ("fit", "pair")
NDEV = 128
SHARES = NDEV // 2
PARTS = len(COLOURS)
KERNEL_VMEM = 28 * 1024 * 1024
LIST = 32
UNROLL = 3
STRIPS_ALWAYS = 4
PARTNERS = ((), (1,), (0,), (0, 1))


def coords(index):
    return index >> 5, (index >> 4) & 1, (index >> 2) & 3, index & 3


def index_of(x, core, z, y):
    return (x << 5) | (core << 4) | (z << 2) | y


def flipped(index, axes, second):
    x, core, z, y = coords(index)
    flip = 3 if (core == 1) != second else 1
    place = [x, z, y]
    for axis in axes:
        place[axis] ^= flip
    return index_of(place[0], core, place[1], place[2])


def axis_pairs(axes, second):
    return [(index, flipped(index, axes, second)) for index in range(NDEV)]


def core_pairs():
    return [(index, index ^ 16) for index in range(NDEV)]


def mirror(index):
    x, core, z, y = coords(index)
    row, col = z * 4 + y, x * 2 + core
    high = row >> 1
    if high < col:
        row, col = 2 * col + (row & 1), high
    elif high > col:
        row, col = 2 * col + 1 - (row & 1), high
    else:
        row ^= 1
    return index_of(col >> 1, col & 1, row >> 2, row & 3)


def bits_of(r, core):
    top, mixed = r >> 1, (r >> 1) ^ (r & 1)
    return jnp.where(core == 0, mixed, top), jnp.where(core == 0, top, mixed)


def row_place(row, core, my_z, my_y):
    z_high, z_low = bits_of((row >> 2) ^ my_z, core)
    y_high, y_low = bits_of((row & 3) ^ my_y, core)
    return z_high * 16 + y_high * 8 + z_low * 2 + y_low


def col_place(col, my_x):
    x_high, x_low = bits_of((col >> 1) ^ my_x, col & 1)
    return x_high * 32 + x_low * 4


def my_place():
    fit, pair = lax.axis_index("fit"), lax.axis_index("pair")
    return fit >> 1, fit & 1, pair >> 2, pair & 3


def packed_place(pair, me):
    my_x, _, my_z, my_y = me
    return row_place(2 * pair + 1, pair & 1, my_z, my_y) + col_place(pair, my_x)


def partial_kernel(mu_hbm, lam_hbm, live_hbm, occ_hbm, ints, coeff, *refs):
    keeps, sends, refs = refs[:PARTS], refs[PARTS : 2 * PARTS], refs[2 * PARTS :]
    (
        ints_v, coeff_v, acc, half, diag, info, mu, lam, live, occ,
        order, first, count, place, ints_sem, coeff_sem, small_sem,
    ) = refs
    slots, fitting = ints.shape[0], ints.shape[1]
    tiles = coeff.shape[0] // BT
    me = my_place()
    my_x, my_core, my_z, my_y = me

    def coeff_copy(b):
        start = pl.multiple_of(occ[b] * OCC, OCC)
        return pltpu.make_async_copy(
            coeff.at[:, pl.ds(start, OCC)], coeff_v.at[:, pl.ds(b * OCC, OCC)], coeff_sem.at[b]
        )

    def ints_copy(t):
        return pltpu.make_async_copy(ints.at[t], ints_v.at[t], ints_sem.at[t])

    small = [
        pltpu.make_async_copy(source, target, small_sem.at[i])
        for i, (source, target) in enumerate(((occ_hbm, occ), (mu_hbm, mu), (live_hbm, live), (lam_hbm, lam)))
    ]
    for copy in small:
        copy.start()
    small[0].wait()
    for b in range(OBLK):
        coeff_copy(b).start()
    for copy in small[1:]:
        copy.wait()

    for m in range(tiles):
        place[m] = 0
    for t in range(slots):
        place[mu[t]] = place[mu[t]] + live[t]
    n_slots, n_tiles = jnp.int32(0), jnp.int32(0)
    for m in range(tiles):
        here = place[m]
        info[n_tiles] = m
        first[n_tiles] = n_slots
        count[n_tiles] = here
        place[m] = n_slots
        n_slots = n_slots + here
        n_tiles = n_tiles + (here > 0).astype(jnp.int32)
    for t in range(slots):
        at = place[mu[t]]
        order[jnp.where(live[t] == 1, at, LIST - 1)] = t
        place[mu[t]] = at + live[t]

    def fetch(s, carry):
        ints_copy(order[s]).start()
        return carry

    lax.fori_loop(0, n_slots, fetch, 0)
    for r in range(tiles):
        name = jnp.where(r < n_tiles, info[r], 0)
        info[r] = name
        info[LIST + r] = row_place(name, 0, my_z, my_y)
        info[2 * LIST + r] = row_place(name, 1, my_z, my_y)
        info[3 * LIST + r] = col_place(name >> 1, my_x)

    for ref in (*keeps, *sends, diag):
        ref[...] = jnp.zeros_like(ref)
    for b in range(OBLK):
        coeff_copy(b).wait()

    def coeff_rows(t):
        return coeff_v[pl.ds(pl.multiple_of(lam[t] * BT, BT), BT), :]

    def one_tile(r, width):
        start, many = first[r], count[r]
        left, right = [], []
        for i in range(width):
            t = order[start + jnp.where(many > i, i, 0)]
            rows = coeff_rows(t)
            left.append(ints_v[t].reshape(fitting * BT, BT))
            right.append(rows if i == 0 else jnp.where(many > i, rows, jnp.zeros_like(rows)))
        value = jnp.dot(
            jnp.concatenate(left, axis=1), jnp.concatenate(right, axis=0), preferred_element_type=jnp.float32
        )
        for p in range(fitting):
            half[r, :, pl.ds(p * OBLK * OCC, OBLK * OCC)] = value[p * BT : (p + 1) * BT].astype(half.dtype)

    def crowded_tile(r):
        acc[...] = jnp.zeros_like(acc)

        def add(s, carry):
            t = order[s]
            acc[...] += jnp.dot(
                ints_v[t].reshape(fitting * BT, BT), coeff_rows(t), preferred_element_type=jnp.float32
            )
            return carry

        lax.fori_loop(first[r], first[r] + count[r], add, 0)
        for p in range(fitting):
            half[r, :, pl.ds(p * OBLK * OCC, OBLK * OCC)] = acc[pl.ds(p * BT, BT), :].astype(half.dtype)

    def some_tiles(k, carry):
        ranks = [jnp.minimum(UNROLL * k + i, n_tiles - 1) for i in range(UNROLL)]

        def arrive(s, inner):
            ints_copy(order[s]).wait()
            return inner

        lax.fori_loop(first[ranks[0]], first[ranks[-1]] + count[ranks[-1]], arrive, 0)
        for r in ranks:
            one_tile(r, 2)
        for r in ranks:

            @pl.when((count[r] > 2) & (count[r] <= 4))
            def _():
                one_tile(r, 4)

            @pl.when(count[r] > 4)
            def _():
                crowded_tile(r)

        return carry

    lax.fori_loop(0, lax.div(n_tiles + UNROLL - 1, UNROLL), some_tiles, 0)

    keep_spare, send_spare = packed_place(my_core, me), packed_place(1 - my_core, me)

    def strip(v):
        left = half[0 : 2 * v + 2].reshape((2 * v + 2) * BT, half.shape[2])
        right = half[2 * v : 2 * v + 2].reshape(2 * BT, half.shape[2])
        value = lax.dot_general(left, right, (((1,), (1,)), ((), ())), preferred_element_type=jnp.float32)
        for j in (2 * v, 2 * v + 1):
            b, valid = info[j], j < n_tiles
            cols = slice((j - 2 * v) * BT, (j - 2 * v + 1) * BT)
            for i in range(j):
                a = info[i]
                mixed = ((a >> 1) != (b >> 1)) & (((a ^ b) & 1) == 1)
                row_rank, col_rank = jnp.where(mixed, j, i), jnp.where(mixed, i, j)
                core = (jnp.where(mixed, a, b) >> 1) & 1
                target = info[LIST * (1 + core) + row_rank] + info[3 * LIST + col_rank]
                keep_at = jnp.where(valid & (core == my_core), target, keep_spare)
                send_at = jnp.where(valid & (core != my_core), target, send_spare)
                for (start, end), keep, send in zip(COLOURS, keeps, sends):
                    block = value[i * BT + start : i * BT + end, cols]
                    keep[keep_at, 0 : end - start, :] = block
                    send[send_at, 0 : end - start, :] = block
            diag[jnp.where(valid, b, tiles)] = value[j * BT : (j + 1) * BT, cols]

    for v in range(tiles // 2):
        if v < STRIPS_ALWAYS:
            strip(v)
        else:
            pl.when(2 * v < n_tiles)(functools.partial(strip, v))

    at_row = lax.broadcasted_iota(jnp.int32, (BT, BT), 0)
    at_col = lax.broadcasted_iota(jnp.int32, (BT, BT), 1)
    for pair in range(tiles // 2):
        even, odd = diag[2 * pair], diag[2 * pair + 1]
        packed = jnp.where(at_row <= at_col, even, odd)
        line = jnp.sum(jnp.where(at_row == at_col, odd, 0.0), axis=0, keepdims=True)
        packed = jnp.concatenate([packed, jnp.broadcast_to(line, (EXTRA, BT))], axis=0)
        target = packed_place(pair, me)
        for ours, refs in ((True, keeps), (False, sends)):

            @pl.when((my_core == pair & 1) == ours)
            def _():
                for (start, end), ref in zip(COLOURS, refs):
                    ref[target] = packed[start : start + ref.shape[1]]


def held(array, space):
    return pltpu.with_memory_space_constraint(array, space)


def partial_sums(ints, tile_mu, tile_lam, tile_live, coefficients, occ_ids):
    slots, fitting = ints.shape[0], ints.shape[1]
    tiles = coefficients.shape[0] // BT
    hbm = pl.BlockSpec(memory_space=pltpu.HBM)
    vmem = pl.BlockSpec(memory_space=pltpu.VMEM)
    shares = [
        pltpu.VMEM((SHARES, end - start + (EXTRA if end == BT else 0), BT), jnp.float32)
        for start, end in COLOURS
    ]
    listed = pltpu.SMEM((LIST,), jnp.int32)
    out = pl.pallas_call(
        partial_kernel,
        out_shape=shares + shares,
        in_specs=[hbm] * 6,
        out_specs=[vmem] * (2 * PARTS),
        scratch_shapes=[
            pltpu.VMEM(ints.shape, ints.dtype),
            pltpu.VMEM((coefficients.shape[0], OBLK * OCC), coefficients.dtype),
            pltpu.VMEM((fitting * BT, OBLK * OCC), jnp.float32),
            pltpu.VMEM((tiles, BT, fitting * OBLK * OCC), jnp.bfloat16),
            pltpu.VMEM((tiles + 1, BT, BT), jnp.float32),
            pltpu.SMEM((4 * LIST,), jnp.int32),
            pltpu.SMEM(tile_mu.shape, jnp.int32),
            pltpu.SMEM(tile_lam.shape, jnp.int32),
            pltpu.SMEM(tile_live.shape, jnp.int32),
            pltpu.SMEM(occ_ids.shape, jnp.int32),
            listed,
            listed,
            listed,
            listed,
            pltpu.SemaphoreType.DMA((slots,)),
            pltpu.SemaphoreType.DMA((OBLK,)),
            pltpu.SemaphoreType.DMA((4,)),
        ],
        compiler_params=pltpu.CompilerParams(vmem_limit_bytes=KERNEL_VMEM),
        cost_estimate=pl.CostEstimate(flops=8 * 10**9, bytes_accessed=5 * 2**20, transcendentals=0),
        name="partial_sums",
    )(*[held(v, pltpu.HBM) for v in (tile_mu, tile_lam, tile_live, occ_ids, ints, coefficients)])
    return out[:PARTS], out[PARTS:]


def finish_kernel(mine, theirs, out, *, scale):
    fit, pair = lax.axis_index("fit"), lax.axis_index("pair")
    high, odd = pair >> 1, pair & 1
    own = lambda: mine[0:BT, :] * scale
    other = lambda: theirs[...] * scale

    @pl.when(high < fit)
    def _():
        for number in range(2):

            @pl.when(odd == number)
            def _():
                out[:, pl.ds(number * BT, BT)] = own()
                out[:, pl.ds((1 - number) * BT, BT)] = other()

    @pl.when(high > fit)
    def _():
        for number in range(2):

            @pl.when(odd == number)
            def _():
                out[:, pl.ds((1 - number) * BT, BT)] = own().T
                out[:, pl.ds(number * BT, BT)] = other().T

    @pl.when(high == fit)
    def _():
        rows = lax.broadcasted_iota(jnp.int32, (BT, BT), 0)
        cols = lax.broadcasted_iota(jnp.int32, (BT, BT), 1)

        @pl.when(odd == 0)
        def _():
            packed = other()
            out[:, 0:BT] = jnp.where(rows <= cols, packed, packed.T)
            out[:, BT:] = own()

        @pl.when(odd == 1)
        def _():
            line = mine[BT : BT + 1, :] * scale
            filled = jnp.where(rows == cols, line, own())
            out[:, 0:BT] = other().T
            out[:, BT:] = jnp.where(rows >= cols, filled, filled.T)


def on_device(ints, tile_mu, tile_lam, tile_live, coefficients, occ_ids):
    count = lax.axis_size("fit") * lax.axis_size("pair")
    scale = 1.0 / math.sqrt(count * ints.shape[1] * OCC * OBLK)

    def swap(array, pairs):
        return lax.ppermute(array, AXES, pairs)

    def after(array, *others):
        return lax.optimization_barrier((array, *others))[0]

    first_bits = (2, 2, 2, NDEV // 16)
    keeps, sends = partial_sums(ints, tile_mu, tile_lam, tile_live, coefficients, occ_ids)
    keeps = [v.reshape(first_bits + v.shape[1:]) for v in keeps]
    cames = [swap(v, core_pairs()).reshape(first_bits + v.shape[1:]) for v in sends]
    tie = ()
    for step in range(3):
        for number in range(PARTS):
            axis = (number + step) % 3
            theirs = after(cames[number], *tie)
            at = lambda v, bit: lax.index_in_dim(v, bit, axis, keepdims=True)
            out_going = at(keeps[number], 1) + at(theirs, 1)
            keeps[number] = at(keeps[number], 0) + at(theirs, 0)
            cames[number] = swap(out_going, axis_pairs((axis,), False))
            tie = (out_going,)
    merged = []
    for mine, theirs in zip(keeps, cames):
        mine = (mine + after(theirs, *tie)).reshape((4, 2) + mine.shape[-2:])
        merged.append(mine)
        tie = (mine,)
    mine = jnp.concatenate(merged, axis=2)

    came = [swap(mine[b], axis_pairs(PARTNERS[b], True)) for b in (3, 2, 1)]
    mine = mine[0] + came[0] + came[1] + came[2]
    own = mine[0] + swap(mine[1], axis_pairs((2,), True))
    other = swap(own[0:BT], [(i, mirror(i)) for i in range(NDEV)])
    return pl.pallas_call(
        functools.partial(finish_kernel, scale=scale),
        out_shape=jax.ShapeDtypeStruct((BT, 2 * BT), jnp.float32),
        name="finish",
    )(held(own, pltpu.VMEM), held(other, pltpu.VMEM))


def solution(mesh):
    return jax.shard_map(
        on_device,
        mesh=mesh,
        in_specs=(
            P(("fit", "pair"), None, None, None),
            P(("fit", "pair")),
            P(("fit", "pair")),
            P(("fit", "pair")),
            P(),
            P(),
        ),
        out_specs=P("pair", "fit"),
        check_vma=False,
    )
```

```python
import functools
import math

import jax
import jax.numpy as jnp
from jax import lax
from jax.experimental import pallas as pl
from jax.experimental.pallas import tpu as pltpu
from jax.sharding import PartitionSpec as P

OCC = 128
OBLK = 2
BT = 128
EXTRA = 8
COLOURS = ((0, 24), (24, 48), (48, 72), (72, 104), (104, 128))
AXES = ("fit", "pair")
NDEV = 128
SHARES = NDEV // 2
PARTS = len(COLOURS)
LATER_ORDER = (0, 1, 2, 4, 3)
KERNEL_VMEM = 28 * 1024 * 1024
LIST = 32
UNROLL = 3
STRIPS_ALWAYS = 4
PARTNERS = ((), (1,), (0,), (0, 1))


def coords(index):
    return index >> 5, (index >> 4) & 1, (index >> 2) & 3, index & 3


def index_of(x, core, z, y):
    return (x << 5) | (core << 4) | (z << 2) | y


def flipped(index, axes, second):
    x, core, z, y = coords(index)
    flip = 3 if (core == 1) != second else 1
    place = [x, z, y]
    for axis in axes:
        place[axis] ^= flip
    return index_of(place[0], core, place[1], place[2])


def axis_pairs(axes, second):
    return [(index, flipped(index, axes, second)) for index in range(NDEV)]


def core_pairs():
    return [(index, index ^ 16) for index in range(NDEV)]


def mirror(index):
    x, core, z, y = coords(index)
    row, col = z * 4 + y, x * 2 + core
    high = row >> 1
    if high < col:
        row, col = 2 * col + (row & 1), high
    elif high > col:
        row, col = 2 * col + 1 - (row & 1), high
    else:
        row ^= 1
    return index_of(col >> 1, col & 1, row >> 2, row & 3)


def bits_of(r, core):
    top, mixed = r >> 1, (r >> 1) ^ (r & 1)
    return jnp.where(core == 0, mixed, top), jnp.where(core == 0, top, mixed)


def row_place(row, core, my_z, my_y):
    z_high, z_low = bits_of((row >> 2) ^ my_z, core)
    y_high, y_low = bits_of((row & 3) ^ my_y, core)
    return z_high * 16 + y_high * 8 + z_low * 2 + y_low


def col_place(col, my_x):
    x_high, x_low = bits_of((col >> 1) ^ my_x, col & 1)
    return x_high * 32 + x_low * 4


def my_place():
    fit, pair = lax.axis_index("fit"), lax.axis_index("pair")
    return fit >> 1, fit & 1, pair >> 2, pair & 3


def packed_place(pair, me):
    my_x, _, my_z, my_y = me
    return row_place(2 * pair + 1, pair & 1, my_z, my_y) + col_place(pair, my_x)


def partial_kernel(mu_hbm, lam_hbm, live_hbm, occ_hbm, ints, coeff, *refs):
    keeps, sends, refs = refs[:PARTS], refs[PARTS : 2 * PARTS], refs[2 * PARTS :]
    (
        ints_v, coeff_v, acc, half, diag, info, mu, lam, live, occ,
        order, first, count, place, ints_sem, coeff_sem, small_sem,
    ) = refs
    slots, fitting = ints.shape[0], ints.shape[1]
    tiles = coeff.shape[0] // BT
    me = my_place()
    my_x, my_core, my_z, my_y = me

    def coeff_copy(b):
        start = pl.multiple_of(occ[b] * OCC, OCC)
        return pltpu.make_async_copy(
            coeff.at[:, pl.ds(start, OCC)], coeff_v.at[:, pl.ds(b * OCC, OCC)], coeff_sem.at[b]
        )

    def ints_copy(t):
        return pltpu.make_async_copy(ints.at[t], ints_v.at[t], ints_sem.at[t])

    small = [
        pltpu.make_async_copy(source, target, small_sem.at[i])
        for i, (source, target) in enumerate(((occ_hbm, occ), (mu_hbm, mu), (live_hbm, live), (lam_hbm, lam)))
    ]
    for copy in small:
        copy.start()
    small[0].wait()
    for b in range(OBLK):
        coeff_copy(b).start()
    for copy in small[1:]:
        copy.wait()

    for m in range(tiles):
        place[m] = 0
    for t in range(slots):
        place[mu[t]] = place[mu[t]] + live[t]
    n_slots, n_tiles = jnp.int32(0), jnp.int32(0)
    for m in range(tiles):
        here = place[m]
        info[n_tiles] = m
        first[n_tiles] = n_slots
        count[n_tiles] = here
        place[m] = n_slots
        n_slots = n_slots + here
        n_tiles = n_tiles + (here > 0).astype(jnp.int32)
    for t in range(slots):
        at = place[mu[t]]
        order[jnp.where(live[t] == 1, at, LIST - 1)] = t
        place[mu[t]] = at + live[t]

    def fetch(s, carry):
        ints_copy(order[s]).start()
        return carry

    lax.fori_loop(0, n_slots, fetch, 0)
    for r in range(tiles):
        name = jnp.where(r < n_tiles, info[r], 0)
        info[r] = name
        info[LIST + r] = row_place(name, 0, my_z, my_y)
        info[2 * LIST + r] = row_place(name, 1, my_z, my_y)
        info[3 * LIST + r] = col_place(name >> 1, my_x)

    for ref in (*keeps, *sends, diag):
        ref[...] = jnp.zeros_like(ref)
    for b in range(OBLK):
        coeff_copy(b).wait()

    def coeff_rows(t):
        return coeff_v[pl.ds(pl.multiple_of(lam[t] * BT, BT), BT), :]

    def one_tile(r, width):
        start, many = first[r], count[r]
        left, right = [], []
        for i in range(width):
            t = order[start + jnp.where(many > i, i, 0)]
            rows = coeff_rows(t)
            left.append(ints_v[t].reshape(fitting * BT, BT))
            right.append(rows if i == 0 else jnp.where(many > i, rows, jnp.zeros_like(rows)))
        value = jnp.dot(
            jnp.concatenate(left, axis=1), jnp.concatenate(right, axis=0), preferred_element_type=jnp.float32
        )
        for p in range(fitting):
            half[r, :, pl.ds(p * OBLK * OCC, OBLK * OCC)] = value[p * BT : (p + 1) * BT].astype(half.dtype)

    def crowded_tile(r):
        acc[...] = jnp.zeros_like(acc)

        def add(s, carry):
            t = order[s]
            acc[...] += jnp.dot(
                ints_v[t].reshape(fitting * BT, BT), coeff_rows(t), preferred_element_type=jnp.float32
            )
            return carry

        lax.fori_loop(first[r], first[r] + count[r], add, 0)
        for p in range(fitting):
            half[r, :, pl.ds(p * OBLK * OCC, OBLK * OCC)] = acc[pl.ds(p * BT, BT), :].astype(half.dtype)

    def some_tiles(k, carry):
        ranks = [jnp.minimum(UNROLL * k + i, n_tiles - 1) for i in range(UNROLL)]

        def arrive(s, inner):
            ints_copy(order[s]).wait()
            return inner

        lax.fori_loop(first[ranks[0]], first[ranks[-1]] + count[ranks[-1]], arrive, 0)
        for r in ranks:
            one_tile(r, 2)
        for r in ranks:

            @pl.when((count[r] > 2) & (count[r] <= 4))
            def _():
                one_tile(r, 4)

            @pl.when(count[r] > 4)
            def _():
                crowded_tile(r)

        return carry

    lax.fori_loop(0, lax.div(n_tiles + UNROLL - 1, UNROLL), some_tiles, 0)

    keep_spare, send_spare = packed_place(my_core, me), packed_place(1 - my_core, me)

    def strip(v):
        left = half[0 : 2 * v + 2].reshape((2 * v + 2) * BT, half.shape[2])
        right = half[2 * v : 2 * v + 2].reshape(2 * BT, half.shape[2])
        value = lax.dot_general(left, right, (((1,), (1,)), ((), ())), preferred_element_type=jnp.float32)
        for j in (2 * v, 2 * v + 1):
            b, valid = info[j], j < n_tiles
            cols = slice((j - 2 * v) * BT, (j - 2 * v + 1) * BT)
            for i in range(j):
                a = info[i]
                mixed = ((a >> 1) != (b >> 1)) & (((a ^ b) & 1) == 1)
                row_rank, col_rank = jnp.where(mixed, j, i), jnp.where(mixed, i, j)
                core = (jnp.where(mixed, a, b) >> 1) & 1
                target = info[LIST * (1 + core) + row_rank] + info[3 * LIST + col_rank]
                keep_at = jnp.where(valid & (core == my_core), target, keep_spare)
                send_at = jnp.where(valid & (core != my_core), target, send_spare)
                for (start, end), keep, send in zip(COLOURS, keeps, sends):
                    block = value[i * BT + start : i * BT + end, cols]
                    keep[keep_at, 0 : end - start, :] = block
                    send[send_at, 0 : end - start, :] = block
            diag[jnp.where(valid, b, tiles)] = value[j * BT : (j + 1) * BT, cols]

    for v in range(tiles // 2):
        if v < STRIPS_ALWAYS:
            strip(v)
        else:
            pl.when(2 * v < n_tiles)(functools.partial(strip, v))

    at_row = lax.broadcasted_iota(jnp.int32, (BT, BT), 0)
    at_col = lax.broadcasted_iota(jnp.int32, (BT, BT), 1)
    for pair in range(tiles // 2):
        even, odd = diag[2 * pair], diag[2 * pair + 1]
        packed = jnp.where(at_row <= at_col, even, odd)
        line = jnp.sum(jnp.where(at_row == at_col, odd, 0.0), axis=0, keepdims=True)
        packed = jnp.concatenate([packed, jnp.broadcast_to(line, (EXTRA, BT))], axis=0)
        target = packed_place(pair, me)
        for ours, refs in ((True, keeps), (False, sends)):

            @pl.when((my_core == pair & 1) == ours)
            def _():
                for (start, end), ref in zip(COLOURS, refs):
                    ref[target] = packed[start : start + ref.shape[1]]


def held(array, space):
    return pltpu.with_memory_space_constraint(array, space)


def partial_sums(ints, tile_mu, tile_lam, tile_live, coefficients, occ_ids):
    slots, fitting = ints.shape[0], ints.shape[1]
    tiles = coefficients.shape[0] // BT
    hbm = pl.BlockSpec(memory_space=pltpu.HBM)
    vmem = pl.BlockSpec(memory_space=pltpu.VMEM)
    shares = [
        pltpu.VMEM((SHARES, end - start + (EXTRA if end == BT else 0), BT), jnp.float32)
        for start, end in COLOURS
    ]
    listed = pltpu.SMEM((LIST,), jnp.int32)
    out = pl.pallas_call(
        partial_kernel,
        out_shape=shares + shares,
        in_specs=[hbm] * 6,
        out_specs=[vmem] * (2 * PARTS),
        scratch_shapes=[
            pltpu.VMEM(ints.shape, ints.dtype),
            pltpu.VMEM((coefficients.shape[0], OBLK * OCC), coefficients.dtype),
            pltpu.VMEM((fitting * BT, OBLK * OCC), jnp.float32),
            pltpu.VMEM((tiles, BT, fitting * OBLK * OCC), jnp.bfloat16),
            pltpu.VMEM((tiles + 1, BT, BT), jnp.float32),
            pltpu.SMEM((4 * LIST,), jnp.int32),
            pltpu.SMEM(tile_mu.shape, jnp.int32),
            pltpu.SMEM(tile_lam.shape, jnp.int32),
            pltpu.SMEM(tile_live.shape, jnp.int32),
            pltpu.SMEM(occ_ids.shape, jnp.int32),
            listed,
            listed,
            listed,
            listed,
            pltpu.SemaphoreType.DMA((slots,)),
            pltpu.SemaphoreType.DMA((OBLK,)),
            pltpu.SemaphoreType.DMA((4,)),
        ],
        compiler_params=pltpu.CompilerParams(vmem_limit_bytes=KERNEL_VMEM),
        cost_estimate=pl.CostEstimate(flops=8 * 10**9, bytes_accessed=5 * 2**20, transcendentals=0),
        name="partial_sums",
    )(*[held(v, pltpu.HBM) for v in (tile_mu, tile_lam, tile_live, occ_ids, ints, coefficients)])
    return out[:PARTS], out[PARTS:]


def finish_kernel(mine, theirs, out, *, scale):
    fit, pair = lax.axis_index("fit"), lax.axis_index("pair")
    high, odd = pair >> 1, pair & 1
    own = lambda: mine[0:BT, :] * scale
    other = lambda: theirs[...] * scale

    @pl.when(high < fit)
    def _():
        for number in range(2):

            @pl.when(odd == number)
            def _():
                out[:, pl.ds(number * BT, BT)] = own()
                out[:, pl.ds((1 - number) * BT, BT)] = other()

    @pl.when(high > fit)
    def _():
        for number in range(2):

            @pl.when(odd == number)
            def _():
                out[:, pl.ds((1 - number) * BT, BT)] = own().T
                out[:, pl.ds(number * BT, BT)] = other().T

    @pl.when(high == fit)
    def _():
        rows = lax.broadcasted_iota(jnp.int32, (BT, BT), 0)
        cols = lax.broadcasted_iota(jnp.int32, (BT, BT), 1)

        @pl.when(odd == 0)
        def _():
            packed = other()
            out[:, 0:BT] = jnp.where(rows <= cols, packed, packed.T)
            out[:, BT:] = own()

        @pl.when(odd == 1)
        def _():
            line = mine[BT : BT + 1, :] * scale
            filled = jnp.where(rows == cols, line, own())
            out[:, 0:BT] = other().T
            out[:, BT:] = jnp.where(rows >= cols, filled, filled.T)


def on_device(ints, tile_mu, tile_lam, tile_live, coefficients, occ_ids):
    count = lax.axis_size("fit") * lax.axis_size("pair")
    scale = 1.0 / math.sqrt(count * ints.shape[1] * OCC * OBLK)

    def swap(array, pairs):
        return lax.ppermute(array, AXES, pairs)

    def after(array, *others):
        return lax.optimization_barrier((array, *others))[0]

    first_bits = (2, 2, 2, NDEV // 16)
    keeps, sends = partial_sums(ints, tile_mu, tile_lam, tile_live, coefficients, occ_ids)
    keeps = [v.reshape(first_bits + v.shape[1:]) for v in keeps]
    cames = [swap(v, core_pairs()).reshape(first_bits + v.shape[1:]) for v in sends]
    tie, sent = (), []
    for step in range(3):
        for number in range(PARTS) if step == 0 else LATER_ORDER:
            axis = (number + step) % 3
            if step == 0:
                tie = tuple(sent[: (number + 1) // 2 * 2 - 1]) if number else ()
            theirs = after(cames[number], *tie)
            at = lambda v, bit: lax.index_in_dim(v, bit, axis, keepdims=True)
            out_going = at(keeps[number], 1) + at(theirs, 1)
            keeps[number] = at(keeps[number], 0) + at(theirs, 0)
            cames[number] = swap(out_going, axis_pairs((axis,), False))
            sent.append(out_going)
            tie = (out_going,)
    merged = [None] * PARTS
    for number in LATER_ORDER:
        mine = keeps[number] + after(cames[number], *tie)
        merged[number] = mine.reshape((4, 2) + mine.shape[-2:])
        tie = (mine,)
    mine = jnp.concatenate(merged, axis=2)

    came = [swap(mine[b], axis_pairs(PARTNERS[b], True)) for b in (3, 2, 1)]
    mine = mine[0] + came[0] + came[1] + came[2]
    own = mine[0] + swap(mine[1], axis_pairs((2,), True))
    other = swap(own[0:BT], [(i, mirror(i)) for i in range(NDEV)])
    return pl.pallas_call(
        functools.partial(finish_kernel, scale=scale),
        out_shape=jax.ShapeDtypeStruct((BT, 2 * BT), jnp.float32),
        name="finish",
    )(held(own, pltpu.VMEM), held(other, pltpu.VMEM))


def solution(mesh):
    return jax.shard_map(
        on_device,
        mesh=mesh,
        in_specs=(
            P(("fit", "pair"), None, None, None),
            P(("fit", "pair")),
            P(("fit", "pair")),
            P(("fit", "pair")),
            P(),
            P(),
        ),
        out_specs=P("pair", "fit"),
        check_vma=False,
    )
```

```python
import functools
import math

import jax
import jax.numpy as jnp
from jax import lax
from jax.experimental import pallas as pl
from jax.experimental.pallas import tpu as pltpu
from jax.sharding import PartitionSpec as P

OCC = 128
OBLK = 2
BT = 128
EXTRA = 8
COLOURS = ((0, 24), (24, 48), (48, 72), (72, 104), (104, 128))
AXES = ("fit", "pair")
NDEV = 128
SHARES = NDEV // 2
PARTS = len(COLOURS)
LATER_ORDER = (0, 1, 2, 4, 3)
KERNEL_VMEM = 28 * 1024 * 1024
LIST = 32
UNROLL = 3
STRIPS_ALWAYS = 4
PARTNERS = ((), (1,), (0,), (0, 1))


def coords(index):
    return index >> 5, (index >> 4) & 1, (index >> 2) & 3, index & 3


def index_of(x, core, z, y):
    return (x << 5) | (core << 4) | (z << 2) | y


def flipped(index, axes, second):
    x, core, z, y = coords(index)
    flip = 3 if (core == 1) != second else 1
    place = [x, z, y]
    for axis in axes:
        place[axis] ^= flip
    return index_of(place[0], core, place[1], place[2])


def axis_pairs(axes, second):
    return [(index, flipped(index, axes, second)) for index in range(NDEV)]


def core_pairs():
    return [(index, index ^ 16) for index in range(NDEV)]


def mirror(index):
    x, core, z, y = coords(index)
    row, col = z * 4 + y, x * 2 + core
    high = row >> 1
    if high < col:
        row, col = 2 * col + (row & 1), high
    elif high > col:
        row, col = 2 * col + 1 - (row & 1), high
    else:
        row ^= 1
    return index_of(col >> 1, col & 1, row >> 2, row & 3)


def bits_of(r, core):
    top, mixed = r >> 1, (r >> 1) ^ (r & 1)
    return jnp.where(core == 0, mixed, top), jnp.where(core == 0, top, mixed)


def row_place(row, core, my_z, my_y):
    z_high, z_low = bits_of((row >> 2) ^ my_z, core)
    y_high, y_low = bits_of((row & 3) ^ my_y, core)
    return z_high * 16 + y_high * 8 + z_low * 2 + y_low


def col_place(col, my_x):
    x_high, x_low = bits_of((col >> 1) ^ my_x, col & 1)
    return x_high * 32 + x_low * 4


def my_place():
    fit, pair = lax.axis_index("fit"), lax.axis_index("pair")
    return fit >> 1, fit & 1, pair >> 2, pair & 3


def packed_place(pair, me):
    my_x, _, my_z, my_y = me
    return row_place(2 * pair + 1, pair & 1, my_z, my_y) + col_place(pair, my_x)


def partial_kernel(mu_hbm, lam_hbm, live_hbm, occ_hbm, ints, coeff, *refs):
    keeps, sends, refs = refs[:PARTS], refs[PARTS : 2 * PARTS], refs[2 * PARTS :]
    (
        ints_v, coeff_v, acc, half, diag, info, mu, lam, live, occ,
        order, first, count, place, ints_sem, coeff_sem, small_sem,
    ) = refs
    slots, fitting = ints.shape[0], ints.shape[1]
    tiles = coeff.shape[0] // BT
    me = my_place()
    my_x, my_core, my_z, my_y = me

    def coeff_copy(b):
        start = pl.multiple_of(occ[b] * OCC, OCC)
        return pltpu.make_async_copy(
            coeff.at[:, pl.ds(start, OCC)], coeff_v.at[:, pl.ds(b * OCC, OCC)], coeff_sem.at[b]
        )

    def ints_copy(t):
        return pltpu.make_async_copy(ints.at[t], ints_v.at[t], ints_sem.at[t])

    small = [
        pltpu.make_async_copy(source, target, small_sem.at[i])
        for i, (source, target) in enumerate(((occ_hbm, occ), (mu_hbm, mu), (live_hbm, live), (lam_hbm, lam)))
    ]
    for copy in small:
        copy.start()
    for ref in (*keeps, *sends, diag):
        ref[...] = jnp.zeros_like(ref)
    small[0].wait()
    for b in range(OBLK):
        coeff_copy(b).start()
    for copy in small[1:]:
        copy.wait()

    for m in range(tiles):
        place[m] = 0
    for t in range(slots):
        place[mu[t]] = place[mu[t]] + live[t]
    n_slots, n_tiles = jnp.int32(0), jnp.int32(0)
    for m in range(tiles):
        here = place[m]
        info[n_tiles] = m
        first[n_tiles] = n_slots
        count[n_tiles] = here
        place[m] = n_slots
        n_slots = n_slots + here
        n_tiles = n_tiles + (here > 0).astype(jnp.int32)
    for t in range(slots):
        at = place[mu[t]]
        order[jnp.where(live[t] == 1, at, LIST - 1)] = t
        place[mu[t]] = at + live[t]

    def fetch(s, carry):
        ints_copy(order[s]).start()
        return carry

    lax.fori_loop(0, n_slots, fetch, 0)
    for r in range(tiles):
        name = jnp.where(r < n_tiles, info[r], 0)
        info[r] = name
        info[LIST + r] = row_place(name, 0, my_z, my_y)
        info[2 * LIST + r] = row_place(name, 1, my_z, my_y)
        info[3 * LIST + r] = col_place(name >> 1, my_x)

    for b in range(OBLK):
        coeff_copy(b).wait()

    def coeff_rows(t):
        return coeff_v[pl.ds(pl.multiple_of(lam[t] * BT, BT), BT), :]

    def one_tile(r, width):
        start, many = first[r], count[r]
        left, right = [], []
        for i in range(width):
            t = order[start + jnp.where(many > i, i, 0)]
            rows = coeff_rows(t)
            left.append(ints_v[t].reshape(fitting * BT, BT))
            right.append(rows if i == 0 else jnp.where(many > i, rows, jnp.zeros_like(rows)))
        value = jnp.dot(
            jnp.concatenate(left, axis=1), jnp.concatenate(right, axis=0), preferred_element_type=jnp.float32
        )
        for p in range(fitting):
            half[r, :, pl.ds(p * OBLK * OCC, OBLK * OCC)] = value[p * BT : (p + 1) * BT].astype(half.dtype)

    def crowded_tile(r):
        acc[...] = jnp.zeros_like(acc)

        def add(s, carry):
            t = order[s]
            acc[...] += jnp.dot(
                ints_v[t].reshape(fitting * BT, BT), coeff_rows(t), preferred_element_type=jnp.float32
            )
            return carry

        lax.fori_loop(first[r], first[r] + count[r], add, 0)
        for p in range(fitting):
            half[r, :, pl.ds(p * OBLK * OCC, OBLK * OCC)] = acc[pl.ds(p * BT, BT), :].astype(half.dtype)

    def some_tiles(k, carry):
        ranks = [jnp.minimum(UNROLL * k + i, n_tiles - 1) for i in range(UNROLL)]

        def arrive(s, inner):
            ints_copy(order[s]).wait()
            return inner

        lax.fori_loop(first[ranks[0]], first[ranks[-1]] + count[ranks[-1]], arrive, 0)
        for r in ranks:
            one_tile(r, 2)
        for r in ranks:

            @pl.when((count[r] > 2) & (count[r] <= 4))
            def _():
                one_tile(r, 4)

            @pl.when(count[r] > 4)
            def _():
                crowded_tile(r)

        return carry

    lax.fori_loop(0, lax.div(n_tiles + UNROLL - 1, UNROLL), some_tiles, 0)

    keep_spare, send_spare = packed_place(my_core, me), packed_place(1 - my_core, me)

    def strip(v):
        left = half[0 : 2 * v + 2].reshape((2 * v + 2) * BT, half.shape[2])
        right = half[2 * v : 2 * v + 2].reshape(2 * BT, half.shape[2])
        value = lax.dot_general(left, right, (((1,), (1,)), ((), ())), preferred_element_type=jnp.float32)
        for j in (2 * v, 2 * v + 1):
            b, valid = info[j], j < n_tiles
            cols = slice((j - 2 * v) * BT, (j - 2 * v + 1) * BT)
            for i in range(j):
                a = info[i]
                mixed = ((a >> 1) != (b >> 1)) & (((a ^ b) & 1) == 1)
                row_rank, col_rank = jnp.where(mixed, j, i), jnp.where(mixed, i, j)
                core = (jnp.where(mixed, a, b) >> 1) & 1
                target = info[LIST * (1 + core) + row_rank] + info[3 * LIST + col_rank]
                keep_at = jnp.where(valid & (core == my_core), target, keep_spare)
                send_at = jnp.where(valid & (core != my_core), target, send_spare)
                for (start, end), keep, send in zip(COLOURS, keeps, sends):
                    block = value[i * BT + start : i * BT + end, cols]
                    keep[keep_at, 0 : end - start, :] = block
                    send[send_at, 0 : end - start, :] = block
            diag[jnp.where(valid, b, tiles)] = value[j * BT : (j + 1) * BT, cols]

    for v in range(tiles // 2):
        if v < STRIPS_ALWAYS:
            strip(v)
        else:
            pl.when(2 * v < n_tiles)(functools.partial(strip, v))

    at_row = lax.broadcasted_iota(jnp.int32, (BT, BT), 0)
    at_col = lax.broadcasted_iota(jnp.int32, (BT, BT), 1)
    for pair in range(tiles // 2):
        even, odd = diag[2 * pair], diag[2 * pair + 1]
        packed = jnp.where(at_row <= at_col, even, odd)
        line = jnp.sum(jnp.where(at_row == at_col, odd, 0.0), axis=0, keepdims=True)
        packed = jnp.concatenate([packed, jnp.broadcast_to(line, (EXTRA, BT))], axis=0)
        target = packed_place(pair, me)
        for ours, refs in ((True, keeps), (False, sends)):

            @pl.when((my_core == pair & 1) == ours)
            def _():
                for (start, end), ref in zip(COLOURS, refs):
                    ref[target] = packed[start : start + ref.shape[1]]


def held(array, space):
    return pltpu.with_memory_space_constraint(array, space)


def partial_sums(ints, tile_mu, tile_lam, tile_live, coefficients, occ_ids):
    slots, fitting = ints.shape[0], ints.shape[1]
    tiles = coefficients.shape[0] // BT
    hbm = pl.BlockSpec(memory_space=pltpu.HBM)
    vmem = pl.BlockSpec(memory_space=pltpu.VMEM)
    shares = [
        pltpu.VMEM((SHARES, end - start + (EXTRA if end == BT else 0), BT), jnp.float32)
        for start, end in COLOURS
    ]
    listed = pltpu.SMEM((LIST,), jnp.int32)
    out = pl.pallas_call(
        partial_kernel,
        out_shape=shares + shares,
        in_specs=[hbm] * 6,
        out_specs=[vmem] * (2 * PARTS),
        scratch_shapes=[
            pltpu.VMEM(ints.shape, ints.dtype),
            pltpu.VMEM((coefficients.shape[0], OBLK * OCC), coefficients.dtype),
            pltpu.VMEM((fitting * BT, OBLK * OCC), jnp.float32),
            pltpu.VMEM((tiles, BT, fitting * OBLK * OCC), jnp.bfloat16),
            pltpu.VMEM((tiles + 1, BT, BT), jnp.float32),
            pltpu.SMEM((4 * LIST,), jnp.int32),
            pltpu.SMEM(tile_mu.shape, jnp.int32),
            pltpu.SMEM(tile_lam.shape, jnp.int32),
            pltpu.SMEM(tile_live.shape, jnp.int32),
            pltpu.SMEM(occ_ids.shape, jnp.int32),
            listed,
            listed,
            listed,
            listed,
            pltpu.SemaphoreType.DMA((slots,)),
            pltpu.SemaphoreType.DMA((OBLK,)),
            pltpu.SemaphoreType.DMA((4,)),
        ],
        compiler_params=pltpu.CompilerParams(vmem_limit_bytes=KERNEL_VMEM),
        cost_estimate=pl.CostEstimate(flops=8 * 10**9, bytes_accessed=5 * 2**20, transcendentals=0),
        name="partial_sums",
    )(*[held(v, pltpu.HBM) for v in (tile_mu, tile_lam, tile_live, occ_ids, ints, coefficients)])
    return out[:PARTS], out[PARTS:]


def finish_kernel(mine, theirs, out, *, scale):
    fit, pair = lax.axis_index("fit"), lax.axis_index("pair")
    high, odd = pair >> 1, pair & 1
    own = lambda: mine[0:BT, :] * scale
    other = lambda: theirs[...] * scale

    @pl.when(high < fit)
    def _():
        for number in range(2):

            @pl.when(odd == number)
            def _():
                out[:, pl.ds(number * BT, BT)] = own()
                out[:, pl.ds((1 - number) * BT, BT)] = other()

    @pl.when(high > fit)
    def _():
        for number in range(2):

            @pl.when(odd == number)
            def _():
                out[:, pl.ds((1 - number) * BT, BT)] = own().T
                out[:, pl.ds(number * BT, BT)] = other().T

    @pl.when(high == fit)
    def _():
        rows = lax.broadcasted_iota(jnp.int32, (BT, BT), 0)
        cols = lax.broadcasted_iota(jnp.int32, (BT, BT), 1)

        @pl.when(odd == 0)
        def _():
            packed = other()
            out[:, 0:BT] = jnp.where(rows <= cols, packed, packed.T)
            out[:, BT:] = own()

        @pl.when(odd == 1)
        def _():
            line = mine[BT : BT + 1, :] * scale
            filled = jnp.where(rows == cols, line, own())
            out[:, 0:BT] = other().T
            out[:, BT:] = jnp.where(rows >= cols, filled, filled.T)


def on_device(ints, tile_mu, tile_lam, tile_live, coefficients, occ_ids):
    count = lax.axis_size("fit") * lax.axis_size("pair")
    scale = 1.0 / math.sqrt(count * ints.shape[1] * OCC * OBLK)

    def swap(array, pairs):
        return lax.ppermute(array, AXES, pairs)

    def after(array, *others):
        return lax.optimization_barrier((array, *others))[0]

    first_bits = (2, 2, 2, NDEV // 16)
    keeps, sends = partial_sums(ints, tile_mu, tile_lam, tile_live, coefficients, occ_ids)
    keeps = [v.reshape(first_bits + v.shape[1:]) for v in keeps]
    cames = [swap(v, core_pairs()).reshape(first_bits + v.shape[1:]) for v in sends]
    tie, sent = (), []
    for step in range(3):
        for number in range(PARTS) if step == 0 else LATER_ORDER:
            axis = (number + step) % 3
            if step == 0:
                tie = tuple(sent[: (number + 1) // 2 * 2 - 1]) if number else ()
            theirs = after(cames[number], *tie)
            at = lambda v, bit: lax.index_in_dim(v, bit, axis, keepdims=True)
            out_going = at(keeps[number], 1) + at(theirs, 1)
            keeps[number] = at(keeps[number], 0) + at(theirs, 0)
            cames[number] = swap(out_going, axis_pairs((axis,), False))
            sent.append(out_going)
            tie = (out_going,)
    merged = [None] * PARTS
    for number in LATER_ORDER:
        mine = keeps[number] + after(cames[number], *tie)
        merged[number] = mine.reshape((4, 2) + mine.shape[-2:])
        tie = (mine,)
    mine = jnp.concatenate(merged, axis=2)

    came = [swap(mine[b], axis_pairs(PARTNERS[b], True)) for b in (3, 2, 1)]
    mine = mine[0] + came[0] + came[1] + came[2]
    own = mine[0] + swap(mine[1], axis_pairs((2,), True))
    other = swap(own[0:BT], [(i, mirror(i)) for i in range(NDEV)])
    return pl.pallas_call(
        functools.partial(finish_kernel, scale=scale),
        out_shape=jax.ShapeDtypeStruct((BT, 2 * BT), jnp.float32),
        name="finish",
    )(held(own, pltpu.VMEM), held(other, pltpu.VMEM))


def solution(mesh):
    return jax.shard_map(
        on_device,
        mesh=mesh,
        in_specs=(
            P(("fit", "pair"), None, None, None),
            P(("fit", "pair")),
            P(("fit", "pair")),
            P(("fit", "pair")),
            P(),
            P(),
        ),
        out_specs=P("pair", "fit"),
        check_vma=False,
    )
```

```python
import functools
import math

import jax
import jax.numpy as jnp
from jax import lax
from jax.experimental import pallas as pl
from jax.experimental.pallas import tpu as pltpu
from jax.sharding import PartitionSpec as P

OCC = 128
OBLK = 2
BT = 128
EXTRA = 8
COLOURS = ((0, 24), (24, 48), (48, 72), (72, 104), (104, 128))
AXES = ("fit", "pair")
NDEV = 128
SHARES = NDEV // 2
PARTS = len(COLOURS)
LATER_ORDER = (0, 1, 2, 4, 3)
KERNEL_VMEM = 28 * 1024 * 1024
LIST = 32
UNROLL = 3
STRIPS_ALWAYS = 5
PARTNERS = ((), (1,), (0,), (0, 1))


def coords(index):
    return index >> 5, (index >> 4) & 1, (index >> 2) & 3, index & 3


def index_of(x, core, z, y):
    return (x << 5) | (core << 4) | (z << 2) | y


def flipped(index, axes, second):
    x, core, z, y = coords(index)
    flip = 3 if (core == 1) != second else 1
    place = [x, z, y]
    for axis in axes:
        place[axis] ^= flip
    return index_of(place[0], core, place[1], place[2])


def axis_pairs(axes, second):
    return [(index, flipped(index, axes, second)) for index in range(NDEV)]


def core_pairs():
    return [(index, index ^ 16) for index in range(NDEV)]


def mirror(index):
    x, core, z, y = coords(index)
    row, col = z * 4 + y, x * 2 + core
    high = row >> 1
    if high < col:
        row, col = 2 * col + (row & 1), high
    elif high > col:
        row, col = 2 * col + 1 - (row & 1), high
    else:
        row ^= 1
    return index_of(col >> 1, col & 1, row >> 2, row & 3)


def bits_of(r, core):
    top, mixed = r >> 1, (r >> 1) ^ (r & 1)
    return jnp.where(core == 0, mixed, top), jnp.where(core == 0, top, mixed)


def row_place(row, core, my_z, my_y):
    z_high, z_low = bits_of((row >> 2) ^ my_z, core)
    y_high, y_low = bits_of((row & 3) ^ my_y, core)
    return z_high * 16 + y_high * 8 + z_low * 2 + y_low


def col_place(col, my_x):
    x_high, x_low = bits_of((col >> 1) ^ my_x, col & 1)
    return x_high * 32 + x_low * 4


def my_place():
    fit, pair = lax.axis_index("fit"), lax.axis_index("pair")
    return fit >> 1, fit & 1, pair >> 2, pair & 3


def packed_place(pair, me):
    my_x, _, my_z, my_y = me
    return row_place(2 * pair + 1, pair & 1, my_z, my_y) + col_place(pair, my_x)


def partial_kernel(mu_hbm, lam_hbm, live_hbm, occ_hbm, ints, coeff, *refs):
    keeps, sends, refs = refs[:PARTS], refs[PARTS : 2 * PARTS], refs[2 * PARTS :]
    (
        ints_v, coeff_v, acc, half, diag, info, mu, lam, live, occ,
        order, first, count, place, ints_sem, coeff_sem, small_sem,
    ) = refs
    slots, fitting = ints.shape[0], ints.shape[1]
    tiles = coeff.shape[0] // BT
    me = my_place()
    my_x, my_core, my_z, my_y = me

    def coeff_copy(b):
        start = pl.multiple_of(occ[b] * OCC, OCC)
        return pltpu.make_async_copy(
            coeff.at[:, pl.ds(start, OCC)], coeff_v.at[:, pl.ds(b * OCC, OCC)], coeff_sem.at[b]
        )

    def ints_copy(t):
        return pltpu.make_async_copy(ints.at[t], ints_v.at[t], ints_sem.at[t])

    small = [
        pltpu.make_async_copy(source, target, small_sem.at[i])
        for i, (source, target) in enumerate(((occ_hbm, occ), (mu_hbm, mu), (live_hbm, live), (lam_hbm, lam)))
    ]
    for copy in small:
        copy.start()
    for ref in (*keeps, *sends, diag):
        ref[...] = jnp.zeros_like(ref)
    small[0].wait()
    for b in range(OBLK):
        coeff_copy(b).start()
    for copy in small[1:]:
        copy.wait()

    for m in range(tiles):
        place[m] = 0
    for t in range(slots):
        place[mu[t]] = place[mu[t]] + live[t]
    n_slots, n_tiles = jnp.int32(0), jnp.int32(0)
    for m in range(tiles):
        here = place[m]
        info[n_tiles] = m
        first[n_tiles] = n_slots
        count[n_tiles] = here
        place[m] = n_slots
        n_slots = n_slots + here
        n_tiles = n_tiles + (here > 0).astype(jnp.int32)
    for t in range(slots):
        at = place[mu[t]]
        order[jnp.where(live[t] == 1, at, LIST - 1)] = t
        place[mu[t]] = at + live[t]

    def fetch(s, carry):
        ints_copy(order[s]).start()
        return carry

    lax.fori_loop(0, n_slots, fetch, 0)
    for r in range(tiles):
        name = jnp.where(r < n_tiles, info[r], 0)
        info[r] = name
        info[LIST + r] = row_place(name, 0, my_z, my_y)
        info[2 * LIST + r] = row_place(name, 1, my_z, my_y)
        info[3 * LIST + r] = col_place(name >> 1, my_x)

    for b in range(OBLK):
        coeff_copy(b).wait()

    def coeff_rows(t):
        return coeff_v[pl.ds(pl.multiple_of(lam[t] * BT, BT), BT), :]

    def one_tile(r, width):
        start, many = first[r], count[r]
        left, right = [], []
        for i in range(width):
            t = order[start + jnp.where(many > i, i, 0)]
            rows = coeff_rows(t)
            left.append(ints_v[t].reshape(fitting * BT, BT))
            right.append(rows if i == 0 else jnp.where(many > i, rows, jnp.zeros_like(rows)))
        value = jnp.dot(
            jnp.concatenate(left, axis=1), jnp.concatenate(right, axis=0), preferred_element_type=jnp.float32
        )
        for p in range(fitting):
            half[r, :, pl.ds(p * OBLK * OCC, OBLK * OCC)] = value[p * BT : (p + 1) * BT].astype(half.dtype)

    def crowded_tile(r):
        acc[...] = jnp.zeros_like(acc)

        def add(s, carry):
            t = order[s]
            acc[...] += jnp.dot(
                ints_v[t].reshape(fitting * BT, BT), coeff_rows(t), preferred_element_type=jnp.float32
            )
            return carry

        lax.fori_loop(first[r], first[r] + count[r], add, 0)
        for p in range(fitting):
            half[r, :, pl.ds(p * OBLK * OCC, OBLK * OCC)] = acc[pl.ds(p * BT, BT), :].astype(half.dtype)

    def some_tiles(k, carry):
        ranks = [jnp.minimum(UNROLL * k + i, n_tiles - 1) for i in range(UNROLL)]

        def arrive(s, inner):
            ints_copy(order[s]).wait()
            return inner

        lax.fori_loop(first[ranks[0]], first[ranks[-1]] + count[ranks[-1]], arrive, 0)
        for r in ranks:
            one_tile(r, 2)
        for r in ranks:

            @pl.when((count[r] > 2) & (count[r] <= 4))
            def _():
                one_tile(r, 4)

            @pl.when(count[r] > 4)
            def _():
                crowded_tile(r)

        return carry

    lax.fori_loop(0, lax.div(n_tiles + UNROLL - 1, UNROLL), some_tiles, 0)

    keep_spare, send_spare = packed_place(my_core, me), packed_place(1 - my_core, me)

    def strip(v):
        left = half[0 : 2 * v + 2].reshape((2 * v + 2) * BT, half.shape[2])
        right = half[2 * v : 2 * v + 2].reshape(2 * BT, half.shape[2])
        value = lax.dot_general(left, right, (((1,), (1,)), ((), ())), preferred_element_type=jnp.float32)
        for j in (2 * v, 2 * v + 1):
            b, valid = info[j], j < n_tiles
            cols = slice((j - 2 * v) * BT, (j - 2 * v + 1) * BT)
            for i in range(j):
                a = info[i]
                mixed = ((a >> 1) != (b >> 1)) & (((a ^ b) & 1) == 1)
                row_rank, col_rank = jnp.where(mixed, j, i), jnp.where(mixed, i, j)
                core = (jnp.where(mixed, a, b) >> 1) & 1
                target = info[LIST * (1 + core) + row_rank] + info[3 * LIST + col_rank]
                keep_at = jnp.where(valid & (core == my_core), target, keep_spare)
                send_at = jnp.where(valid & (core != my_core), target, send_spare)
                for (start, end), keep, send in zip(COLOURS, keeps, sends):
                    block = value[i * BT + start : i * BT + end, cols]
                    keep[keep_at, 0 : end - start, :] = block
                    send[send_at, 0 : end - start, :] = block
            diag[jnp.where(valid, b, tiles)] = value[j * BT : (j + 1) * BT, cols]

    for v in range(tiles // 2):
        if v < STRIPS_ALWAYS:
            strip(v)
        else:
            pl.when(2 * v < n_tiles)(functools.partial(strip, v))

    at_row = lax.broadcasted_iota(jnp.int32, (BT, BT), 0)
    at_col = lax.broadcasted_iota(jnp.int32, (BT, BT), 1)
    for pair in range(tiles // 2):
        even, odd = diag[2 * pair], diag[2 * pair + 1]
        packed = jnp.where(at_row <= at_col, even, odd)
        line = jnp.sum(jnp.where(at_row == at_col, odd, 0.0), axis=0, keepdims=True)
        packed = jnp.concatenate([packed, jnp.broadcast_to(line, (EXTRA, BT))], axis=0)
        target = packed_place(pair, me)
        for ours, refs in ((True, keeps), (False, sends)):

            @pl.when((my_core == pair & 1) == ours)
            def _():
                for (start, end), ref in zip(COLOURS, refs):
                    ref[target] = packed[start : start + ref.shape[1]]


def held(array, space):
    return pltpu.with_memory_space_constraint(array, space)


def partial_sums(ints, tile_mu, tile_lam, tile_live, coefficients, occ_ids):
    slots, fitting = ints.shape[0], ints.shape[1]
    tiles = coefficients.shape[0] // BT
    hbm = pl.BlockSpec(memory_space=pltpu.HBM)
    vmem = pl.BlockSpec(memory_space=pltpu.VMEM)
    shares = [
        pltpu.VMEM((SHARES, end - start + (EXTRA if end == BT else 0), BT), jnp.float32)
        for start, end in COLOURS
    ]
    listed = pltpu.SMEM((LIST,), jnp.int32)
    out = pl.pallas_call(
        partial_kernel,
        out_shape=shares + shares,
        in_specs=[hbm] * 6,
        out_specs=[vmem] * (2 * PARTS),
        scratch_shapes=[
            pltpu.VMEM(ints.shape, ints.dtype),
            pltpu.VMEM((coefficients.shape[0], OBLK * OCC), coefficients.dtype),
            pltpu.VMEM((fitting * BT, OBLK * OCC), jnp.float32),
            pltpu.VMEM((tiles, BT, fitting * OBLK * OCC), jnp.bfloat16),
            pltpu.VMEM((tiles + 1, BT, BT), jnp.float32),
            pltpu.SMEM((4 * LIST,), jnp.int32),
            pltpu.SMEM(tile_mu.shape, jnp.int32),
            pltpu.SMEM(tile_lam.shape, jnp.int32),
            pltpu.SMEM(tile_live.shape, jnp.int32),
            pltpu.SMEM(occ_ids.shape, jnp.int32),
            listed,
            listed,
            listed,
            listed,
            pltpu.SemaphoreType.DMA((slots,)),
            pltpu.SemaphoreType.DMA((OBLK,)),
            pltpu.SemaphoreType.DMA((4,)),
        ],
        compiler_params=pltpu.CompilerParams(vmem_limit_bytes=KERNEL_VMEM),
        cost_estimate=pl.CostEstimate(flops=8 * 10**9, bytes_accessed=5 * 2**20, transcendentals=0),
        name="partial_sums",
    )(*[held(v, pltpu.HBM) for v in (tile_mu, tile_lam, tile_live, occ_ids, ints, coefficients)])
    return out[:PARTS], out[PARTS:]


def finish_kernel(mine, theirs, out, *, scale):
    fit, pair = lax.axis_index("fit"), lax.axis_index("pair")
    high, odd = pair >> 1, pair & 1
    own = lambda: mine[0:BT, :] * scale
    other = lambda: theirs[...] * scale

    @pl.when(high < fit)
    def _():
        for number in range(2):

            @pl.when(odd == number)
            def _():
                out[:, pl.ds(number * BT, BT)] = own()
                out[:, pl.ds((1 - number) * BT, BT)] = other()

    @pl.when(high > fit)
    def _():
        for number in range(2):

            @pl.when(odd == number)
            def _():
                out[:, pl.ds((1 - number) * BT, BT)] = own().T
                out[:, pl.ds(number * BT, BT)] = other().T

    @pl.when(high == fit)
    def _():
        rows = lax.broadcasted_iota(jnp.int32, (BT, BT), 0)
        cols = lax.broadcasted_iota(jnp.int32, (BT, BT), 1)

        @pl.when(odd == 0)
        def _():
            packed = other()
            out[:, 0:BT] = jnp.where(rows <= cols, packed, packed.T)
            out[:, BT:] = own()

        @pl.when(odd == 1)
        def _():
            line = mine[BT : BT + 1, :] * scale
            filled = jnp.where(rows == cols, line, own())
            out[:, 0:BT] = other().T
            out[:, BT:] = jnp.where(rows >= cols, filled, filled.T)


def on_device(ints, tile_mu, tile_lam, tile_live, coefficients, occ_ids):
    count = lax.axis_size("fit") * lax.axis_size("pair")
    scale = 1.0 / math.sqrt(count * ints.shape[1] * OCC * OBLK)

    def swap(array, pairs):
        return lax.ppermute(array, AXES, pairs)

    def after(array, *others):
        return lax.optimization_barrier((array, *others))[0]

    first_bits = (2, 2, 2, NDEV // 16)
    keeps, sends = partial_sums(ints, tile_mu, tile_lam, tile_live, coefficients, occ_ids)
    keeps = [v.reshape(first_bits + v.shape[1:]) for v in keeps]
    cames = [swap(v, core_pairs()).reshape(first_bits + v.shape[1:]) for v in sends]
    tie, sent = (), []
    for step in range(3):
        for number in range(PARTS) if step == 0 else LATER_ORDER:
            axis = (number + step) % 3
            if step == 0:
                tie = tuple(sent[: (number + 1) // 2 * 2 - 1]) if number else ()
            theirs = after(cames[number], *tie)
            at = lambda v, bit: lax.index_in_dim(v, bit, axis, keepdims=True)
            out_going = at(keeps[number], 1) + at(theirs, 1)
            keeps[number] = at(keeps[number], 0) + at(theirs, 0)
            cames[number] = swap(out_going, axis_pairs((axis,), False))
            sent.append(out_going)
            tie = (out_going,)
    merged = [None] * PARTS
    for number in LATER_ORDER:
        mine = keeps[number] + after(cames[number], *tie)
        merged[number] = mine.reshape((4, 2) + mine.shape[-2:])
        tie = (mine,)
    mine = jnp.concatenate(merged, axis=2)

    came = [swap(mine[b], axis_pairs(PARTNERS[b], True)) for b in (3, 2, 1)]
    mine = mine[0] + came[0] + came[1] + came[2]
    own = mine[0] + swap(mine[1], axis_pairs((2,), True))
    other = swap(own[0:BT], [(i, mirror(i)) for i in range(NDEV)])
    return pl.pallas_call(
        functools.partial(finish_kernel, scale=scale),
        out_shape=jax.ShapeDtypeStruct((BT, 2 * BT), jnp.float32),
        name="finish",
    )(held(own, pltpu.VMEM), held(other, pltpu.VMEM))


def solution(mesh):
    return jax.shard_map(
        on_device,
        mesh=mesh,
        in_specs=(
            P(("fit", "pair"), None, None, None),
            P(("fit", "pair")),
            P(("fit", "pair")),
            P(("fit", "pair")),
            P(),
            P(),
        ),
        out_specs=P("pair", "fit"),
        check_vma=False,
    )
```
